128 devices in a mesh: section: 16 (over z, x_lo, core), dp: 8 (over y, x_hi).
Axes of the slice: x: 4 (x_hi: 2, x_lo: 2; x = x_hi * 2 + x_lo), y: 4, z: 4, core: 2. Of those that a mesh axis runs over, the one named last changes fastest.
Arguments:
- weight_old: bfloat16 [3072, 3072], P('section'), may hold values from -0.109375 to 0.109375
- moment_one: float32 [3072, 3072], P('section'), may hold values from -3 to 3
- moment_two: float32 [3072, 3072], P('section'), may hold values from 0.05 to 2
- residual_old: bfloat16 [8, 3072, 3072], P('dp', 'section'), may hold values from -4 to 4
- grads: bfloat16 [8, 16, 384, 3072], P('dp', 'section'), may hold values from -6 to 6
- exponents: int32 [8, 16, 384, 12], P('dp', 'section'), may hold values from -1 to 1
Outputs:
- new_weight: bfloat16 [16, 384, 3072], P('section')
- new_moment_one: float32 [16, 384, 3072], P('section')
- new_moment_two: float32 [16, 384, 3072], P('section')
- new_residual: bfloat16 [8, 16, 384, 3072], P('dp', 'section')
The draws below stay inside these ranges and needn't reach their ends.
All inputs are finite; a program needn't handle non-finite values.
Results may differ from the reference program's by a relative error of at most 0.0075.
Values may be sent and summed in bfloat16 or wider, within the bound.
No kernel may reach another device: no remote copies, remote signals or barrier semaphores. Data moves between devices by JAX's collectives and lax.ppermute only.
A program may use at most 128 MiB of HBM per device.

```python
import math
import jax
import jax.numpy as jnp
from jax import lax

COLS = 3072
BLOCK = 256
SECTIONS = 16
REPLICAS = 8
ROWS = 3072
GROWS = 384
NSCALE = 12


def plant(drawn, stream_key, low, top_value):
    longest = drawn.shape.index(max(drawn.shape))
    spots = []
    for shift in (0, 1):
        where = [jax.random.randint(jax.random.fold_in(stream_key, axis), (), 0, length) for axis, length in enumerate(drawn.shape)]
        where[longest] = (where[longest] + shift) % drawn.shape[longest]
        spots.append(tuple(where))
    return drawn.at[spots[0]].set(low).at[spots[1]].set(top_value)


def block_scale(key, extent, pieces, smallest, largest):
    gain = 1.0
    for dim, parts in pieces:
        heights = jax.random.uniform(jax.random.fold_in(jax.random.fold_in(key, 6), dim), (parts,), jnp.float32, smallest / len(pieces), largest / len(pieces))
        gain = gain * jnp.repeat(jnp.exp(heights), extent[dim] // parts).reshape((-1,) + (1,) * (len(extent) - 1 - dim))
    return gain


def centred(rng, shape, width, most, shards=(), dtype=jnp.bfloat16):
    loudness = block_scale(rng, shape, shards, -0.22, 0.18) if shards else 1.0
    values = jax.random.normal(rng, shape, jnp.float32) * width * loudness
    return jnp.minimum(jnp.maximum(values, -most), most).astype(dtype)


def setup_inputs(seed: int = 0) -> dict:
    seeds = jax.random.split(jax.random.key(seed), 7)
    weight_old = centred(seeds[0], (ROWS, COLS), ROWS ** -0.5, 0.109375, ((0, 16),))
    moment_one = centred(seeds[1], (ROWS, COLS), 0.3, 3.0, ((0, 16),), jnp.float32)
    moment_two = jnp.clip(jnp.exp(math.log(2.0) - 3.6888794 * jax.random.uniform(seeds[2], (ROWS, COLS), jnp.float32) ** block_scale(seeds[2], (ROWS, COLS), ((0, 16),), -0.2, 0.2)), 0.05, 2.0)
    residual_old = centred(seeds[3], (REPLICAS, ROWS, COLS), 0.5, 4.0, ((0, 8), (1, 16)))
    grads = centred(seeds[4], (REPLICAS, SECTIONS, GROWS, COLS), 1.0, 6.0, ((0, 8), (1, 16)))
    exponents = plant(jax.random.randint(seeds[5], (REPLICAS, SECTIONS, GROWS, NSCALE), -1, 2), jax.random.fold_in(seeds[5], 1), -1, 1).astype(jnp.int32)
    return {"weight_old": weight_old, "moment_one": moment_one, "moment_two": moment_two, "residual_old": residual_old, "grads": grads, "exponents": exponents}


BETA_ONE = 0.9
BETA_TWO = 0.95
LEARN_RATE = 0.001
EPSILON = 1e-08
BIAS_ONE = 1.0 - 0.9 ** 10
BIAS_TWO = 1.0 - 0.95 ** 10

def adam_update(weight, moment_a, moment_b, averaged):
    moment_a = BETA_ONE * moment_a + (1.0 - BETA_ONE) * averaged
    moment_b = BETA_TWO * moment_b + (1.0 - BETA_TWO) * averaged * averaged
    update = LEARN_RATE * (moment_a / BIAS_ONE) / (jnp.sqrt(moment_b / BIAS_TWO) + EPSILON)
    return ((weight.astype(jnp.float32) - update).astype(jnp.bfloat16), moment_a, moment_b)

def reference(weight_old, moment_one, moment_two, residual_old, grads, exponents):
    groups = SECTIONS // 2
    carried = residual_old.astype(jnp.float32).reshape(REPLICAS, groups, GROWS, COLS)
    carried = jnp.repeat(carried, 2, axis=1)
    summand = grads.astype(jnp.float32) + carried
    scales = jnp.exp2(exponents.astype(jnp.float32))[..., None]
    blocks = summand.reshape(REPLICAS, SECTIONS, GROWS, NSCALE, BLOCK)
    clipped = jnp.clip(blocks, -scales, scales).reshape(summand.shape).astype(jnp.bfloat16)
    new_residual = (summand - clipped.astype(jnp.float32)).astype(jnp.bfloat16)
    summed = lax.optimization_barrier(jnp.sum(clipped.astype(jnp.float32).reshape(REPLICAS, groups, 2, GROWS, COLS), axis=(0, 2)))
    averaged = (summed / (2 * REPLICAS)).reshape(ROWS, COLS)
    updated, moment_a, moment_b = adam_update(weight_old, moment_one, moment_two, averaged)

    def expand(values):
        return jnp.repeat(values.reshape(groups, GROWS, COLS), 2, axis=0)
    return (expand(updated), expand(moment_a), expand(moment_b), new_residual)
```

```python
import functools

import jax
import jax.numpy as jnp
from jax import lax
from jax.experimental import pallas as pl
from jax.experimental.pallas import tpu as pltpu
from jax.sharding import PartitionSpec as P

BETA_ONE = 0.9
BETA_TWO = 0.95
LEARN_RATE = 0.001
EPSILON = 1e-08
BIAS_ONE = 1.0 - 0.9**10
BIAS_TWO = 1.0 - 0.95**10
BLOCK = 256
STEP = 48
F32 = jnp.float32
BF16 = jnp.bfloat16


def swapped(value):
    pairs = [(source, source ^ 1) for source in range(lax.axis_size("section"))]
    return lax.ppermute(value, "section", pairs)


def clipped_block(grads, residual, scales, block):
    columns = slice(block * BLOCK, (block + 1) * BLOCK)
    summand = grads[:, columns].astype(F32) + residual[:, columns].astype(F32)
    scale = scales[:, block : block + 1]
    return summand, jnp.clip(summand, -scale, scale).astype(BF16), columns


def own_kernel(half, grads, residual, scales, clipped, left):
    for block in range(grads.shape[1] // BLOCK):
        summand, kept, columns = clipped_block(grads, residual, scales, block)
        clipped[:, columns] = kept
        left[:, columns] = (summand - kept.astype(F32)).astype(BF16)


def other_kernel(half, grads, residual, scales, held, left):
    for block in range(grads.shape[1] // BLOCK):
        summand, kept, columns = clipped_block(grads, residual, scales, block)
        left[:, columns] = (summand - kept.astype(F32)).astype(BF16)


def pair_kernel(grads, residual, scales, clipped, summed):
    width = summed.shape[2]
    for block in range(grads.shape[1] // BLOCK):
        _, kept, columns = clipped_block(grads, residual, scales, block)
        total = (kept.astype(F32) + clipped[:, columns].astype(F32)).astype(BF16)
        for part in range(BLOCK // 128):
            start = block * BLOCK + part * 128
            at = start % width
            summed[start // width, :, at : at + 128] = total[:, part * 128 : (part + 1) * 128]


def sum_kernel(parts, out):
    total = parts[0].astype(F32)
    for part in range(1, parts.shape[0]):
        total = total + parts[part].astype(F32)
    total = total.astype(BF16)
    for part in range(out.shape[0]):
        out[part] = total


def adam_kernel(half, summed, weight, moment_one, moment_two, *rest):
    new_weight, new_one, new_two = rest[-3:]
    replicas = 16.0
    for part in range(summed.shape[0]):
        width = summed.shape[2]
        columns = slice(part * width, (part + 1) * width)
        averaged = summed[part].astype(F32) / replicas
        moment_a = BETA_ONE * moment_one[:, columns] + (1.0 - BETA_ONE) * averaged
        moment_b = BETA_TWO * moment_two[:, columns] + (1.0 - BETA_TWO) * averaged * averaged
        update = LEARN_RATE * (moment_a / BIAS_ONE) / (jnp.sqrt(moment_b / BIAS_TWO) + EPSILON)
        new_weight[:, columns] = (weight[:, columns].astype(F32) - update).astype(BF16)
        new_one[:, columns] = moment_a
        new_two[:, columns] = moment_b


def cost(flops, moved):
    return pl.CostEstimate(flops=flops, bytes_accessed=moved, transcendentals=0)


def rows_of(half_rows):
    steps = half_rows // STEP
    return steps, lambda step, half: (half[0] * steps + step, 0)


def clip_half(half, grads, residual, scales, left_held):
    rows, columns = residual.shape
    steps, at_half = rows_of(rows)
    at_step = lambda step, half: (step, 0)
    in_specs = [
        pl.BlockSpec((STEP, columns), at_half),
        pl.BlockSpec((STEP, columns), at_step),
        pl.BlockSpec((STEP, scales.shape[1]), at_half),
    ]
    left_spec = pl.BlockSpec((STEP, columns), at_half)
    left_shape = jax.ShapeDtypeStruct(grads.shape, BF16)
    size = rows * columns
    if left_held is None:
        return pl.pallas_call(
            own_kernel,
            grid_spec=pltpu.PrefetchScalarGridSpec(
                num_scalar_prefetch=1,
                grid=(steps,),
                in_specs=in_specs,
                out_specs=[pl.BlockSpec((STEP, columns), at_step), left_spec],
            ),
            out_shape=[jax.ShapeDtypeStruct((rows, columns), BF16), left_shape],
            cost_estimate=cost(6 * size, 8 * size),
            name="clip_own",
        )(half, grads, residual, scales)
    return pl.pallas_call(
        other_kernel,
        grid_spec=pltpu.PrefetchScalarGridSpec(
            num_scalar_prefetch=1,
            grid=(steps,),
            in_specs=in_specs + [pl.BlockSpec(memory_space=pl.ANY)],
            out_specs=left_spec,
        ),
        out_shape=left_shape,
        input_output_aliases={4: 0},
        cost_estimate=cost(6 * size, 6 * size),
        name="clip_other",
    )(half, grads, residual, scales, left_held)


def pair_sum(grads, residual, scales, clipped, parts):
    rows, columns = residual.shape
    at_step = lambda step: (step, 0)
    spec = pl.BlockSpec((STEP, columns), at_step)
    size = rows * columns
    return pl.pallas_call(
        pair_kernel,
        grid=(rows // STEP,),
        in_specs=[spec, spec, pl.BlockSpec((STEP, scales.shape[1]), at_step), spec],
        out_specs=pl.BlockSpec((parts, STEP, columns // parts), lambda step: (0, step, 0)),
        out_shape=jax.ShapeDtypeStruct((parts, rows, columns // parts), BF16),
        cost_estimate=cost(6 * size, 8 * size),
        name="pair_sum",
    )(grads, residual, scales, clipped)


def replica_sum(parts):
    count, rows, columns = parts.shape
    spec = pl.BlockSpec((count, STEP, columns), lambda step: (0, step, 0))
    return pl.pallas_call(
        sum_kernel,
        grid=(rows // STEP,),
        in_specs=[spec],
        out_specs=spec,
        out_shape=jax.ShapeDtypeStruct(parts.shape, BF16),
        cost_estimate=cost(count * rows * columns, 4 * count * rows * columns),
        name="replica_sum",
    )(parts)


def adam_half(half, summed, weight, moment_one, moment_two, held):
    parts, rows, width = summed.shape
    columns = parts * width
    steps, at_half = rows_of(rows)
    at_step = lambda step, half: (step, 0)
    spec = pl.BlockSpec((STEP, columns), at_step)
    any_spec = pl.BlockSpec(memory_space=pl.ANY)
    out_spec = pl.BlockSpec((STEP, columns), at_half)
    size = rows * columns
    return pl.pallas_call(
        adam_kernel,
        grid_spec=pltpu.PrefetchScalarGridSpec(
            num_scalar_prefetch=1,
            grid=(steps,),
            in_specs=[pl.BlockSpec((parts, STEP, width), lambda step, half: (0, step, 0))]
            + [spec] * 3
            + [any_spec] * len(held),
            out_specs=[out_spec] * 3,
        ),
        out_shape=[jax.ShapeDtypeStruct((2 * rows, columns), kind) for kind in (BF16, F32, F32)],
        input_output_aliases={5 + at: at for at in range(len(held))},
        cost_estimate=cost(20 * size, 22 * size),
        name="adam_half",
    )(half, summed, weight, moment_one, moment_two, *held)


def shards(weight_old, moment_one, moment_two, residual_old, grads, exponents):
    parity = lax.axis_index("section") % 2
    own = parity.astype(jnp.int32).reshape(1)
    other = 1 - own
    replicas = lax.axis_size("dp")
    residual = residual_old[0]
    grads = grads[0, 0]
    rows = residual.shape[0]
    scales = jnp.exp2(exponents[0, 0].astype(F32))

    partner_grads, partner_scales = swapped(
        (
            lax.dynamic_slice_in_dim(grads, other[0] * rows, rows, axis=0),
            lax.dynamic_slice_in_dim(scales, other[0] * rows, rows, axis=0),
        )
    )
    partner_residual = swapped(residual)
    clipped, left = clip_half(own, grads, residual, scales, None)
    paired = pair_sum(partner_grads, residual, partner_scales, clipped, replicas)
    partner_one, partner_two, partner_weight = swapped((moment_one, moment_two, weight_old))

    scattered = lax.all_to_all(paired, "dp", 0, 0, tiled=True)
    summed = lax.all_to_all(replica_sum(scattered), "dp", 0, 0, tiled=True)
    partner_summed = swapped(summed)
    left = clip_half(other, grads, partner_residual, scales, left)
    updated = adam_half(own, summed, weight_old, moment_one, moment_two, ())
    updated = adam_half(
        other, partner_summed, partner_weight, partner_one, partner_two, tuple(updated)
    )
    return (updated[0][None], updated[1][None], updated[2][None], left[None, None])


def solution(mesh):
    in_specs = (
        P("section", None),
        P("section", None),
        P("section", None),
        P("dp", "section", None),
        P("dp", "section", None, None),
        P("dp", "section", None, None),
    )
    out_specs = (
        P("section", None, None),
        P("section", None, None),
        P("section", None, None),
        P("dp", "section", None, None),
    )
    return jax.shard_map(shards, mesh=mesh, in_specs=in_specs, out_specs=out_specs, check_vma=False)
```

```python
import functools

import jax
import jax.numpy as jnp
from jax import lax
from jax.experimental import pallas as pl
from jax.experimental.pallas import tpu as pltpu
from jax.sharding import PartitionSpec as P

BETA_ONE = 0.9
BETA_TWO = 0.95
LEARN_RATE = 0.001
EPSILON = 1e-08
BIAS_ONE = 1.0 - 0.9**10
BIAS_TWO = 1.0 - 0.95**10
BLOCK = 256
PIECES = 3
LANES = 128
OWN_STEPS = 4
VMEM_LIMIT = 12 * 2**20
F32 = jnp.float32
BF16 = jnp.bfloat16
IN_VMEM = pl.BlockSpec(memory_space=pltpu.VMEM)
IN_HBM = pl.BlockSpec(memory_space=pltpu.HBM)


def core_swap(value):
    pairs = [(source, source ^ 1) for source in range(lax.axis_size("section"))]
    return lax.ppermute(value, "section", pairs)


def cube_swap(value, dim):
    count = lax.axis_size("dp")
    if dim == 0:
        pairs = [(source, source ^ 2) for source in range(count)]
    elif dim == 1:
        pairs = [(source, (3 - source // 2) * 2 + source % 2) for source in range(count)]
    else:
        pairs = [(source, source ^ 1) for source in range(count)]
    return lax.ppermute(value, "dp", pairs)


def core_parity():
    return lax.axis_index("section").astype(jnp.int32) % 2


def cube_bits():
    replica = lax.axis_index("dp").astype(jnp.int32)
    y = replica // 2
    return [((y + 1) // 2) % 2, y // 2, replica % 2]


class HbmOut(tuple):
    pass


def call(body, outs, operands, flops, moved, name, scratch=(), aliases=None, in_hbm=0):
    near = operands[: len(operands) - in_hbm]
    far = operands[len(operands) - in_hbm :]
    return pl.pallas_call(
        body,
        in_specs=[IN_VMEM] * len(near) + [IN_HBM] * in_hbm,
        out_specs=[IN_HBM if isinstance(out, HbmOut) else IN_VMEM for out in outs],
        out_shape=[
            (pltpu.HBM if isinstance(out, HbmOut) else pltpu.VMEM)(out[0], out[1]) for out in outs
        ],
        scratch_shapes=list(scratch),
        input_output_aliases=aliases or {},
        compiler_params=pltpu.CompilerParams(vmem_limit_bytes=VMEM_LIMIT),
        cost_estimate=pl.CostEstimate(flops=flops, bytes_accessed=moved, transcendentals=0),
        name=name,
    )(
        *[pltpu.with_memory_space_constraint(value, pltpu.VMEM) for value in near],
        *[pltpu.with_memory_space_constraint(value, pltpu.HBM) for value in far],
    )


def aligned(start, size):
    return pl.ds(pl.multiple_of(start, 32), size)


def message_kernel(exponents, grads, message, scales, read, turned, sems):
    rows, columns = message.shape[0], grads.shape[1]
    base = (1 - core_parity()) * rows
    part = rows // 4
    first = pltpu.make_async_copy(exponents, read, sems.at[4])
    first.start()
    copies = []
    for at in range(4):
        copies.append(
            pltpu.make_async_copy(
                grads.at[aligned(base + at * part, part)],
                message.at[pl.ds(at * part, part), pl.ds(0, columns)],
                sems.at[at],
            )
        )
        copies[-1].start()
    turned[...] = jnp.zeros_like(turned)
    first.wait()
    for block in range(exponents.shape[0]):
        turned[block : block + 1, :] = read[block].astype(F32)
    scales[...] = jnp.exp2(turned[...].T).astype(BF16)
    message[:, columns:] = scales[aligned(base, rows), :]
    for copy in copies:
        copy.wait()


def make_message(exponents, grads, rows):
    blocks, _, all_rows = exponents.shape
    columns = grads.shape[1]
    return call(
        message_kernel,
        [((rows, columns + LANES), BF16), ((all_rows, LANES), BF16)],
        [exponents, grads],
        0,
        2 * rows * columns,
        "make_message",
        scratch=[
            pltpu.VMEM(exponents.shape, exponents.dtype),
            pltpu.VMEM((LANES, all_rows), F32),
            pltpu.SemaphoreType.DMA((5,)),
        ],
        in_hbm=2,
    )


def own_kernel(scales, grads, residual, clipped, carried, read, sems):
    rows, columns = residual.shape
    base = core_parity() * rows
    part = rows // OWN_STEPS
    copies = []
    for step in range(OWN_STEPS):
        here = pl.ds(step * part, part)
        there = aligned(base + step * part, part)
        copies.append(
            (
                pltpu.make_async_copy(grads.at[there], read.at[here], sems.at[0, step]),
                pltpu.make_async_copy(residual.at[here], carried.at[here], sems.at[1, step]),
            )
        )
        for copy in copies[-1]:
            copy.start()
    for step in range(OWN_STEPS):
        for copy in copies[step]:
            copy.wait()
        here = slice(step * part, (step + 1) * part)
        scale = scales[aligned(base + step * part, part), :]
        for block in range(columns // BLOCK):
            at = slice(block * BLOCK, (block + 1) * BLOCK)
            limit = scale[:, block : block + 1]
            clipped[here, at] = jnp.clip(read[here, at] + carried[here, at], -limit, limit)


def clip_own(scales, grads, residual):
    rows, columns = residual.shape
    return call(
        own_kernel,
        [(residual.shape, BF16)] * 2,
        [scales, grads, residual],
        4 * rows * columns,
        4 * rows * columns,
        "clip_own",
        scratch=[pltpu.VMEM(residual.shape, BF16), pltpu.SemaphoreType.DMA((2, OWN_STEPS))],
        in_hbm=2,
    )


def pair_kernel(clipped, residual, message, *outs):
    rows, columns = residual.shape
    half, width = rows // 2, columns // PIECES
    for piece in range(PIECES):
        bit = cube_bits()[piece]
        for out, start in ((outs[piece], 1 - bit), (outs[PIECES + piece], bit)):
            here = aligned(start * half, half)
            scale = message[here, columns:]
            for block in range(piece * width // BLOCK, (piece + 1) * width // BLOCK):
                at = slice(block * BLOCK, (block + 1) * BLOCK)
                to = slice(block * BLOCK - piece * width, (block + 1) * BLOCK - piece * width)
                limit = scale[:, block : block + 1]
                partner = jnp.clip(message[here, at] + residual[here, at], -limit, limit)
                out[:, to] = clipped[here, at] + partner


def pair_sums(clipped, residual, message):
    rows, columns = residual.shape
    size = rows * columns
    outs = call(
        pair_kernel,
        [((rows // 2, columns // PIECES), BF16)] * (2 * PIECES),
        [clipped, residual, message],
        5 * size,
        size,
        "pair_sums",
    )
    return outs[:PIECES], outs[PIECES:]


def add_kernel(*refs):
    for mine, theirs, out in zip(refs[:PIECES], refs[PIECES : 2 * PIECES], refs[2 * PIECES :]):
        out[...] = mine[...] + theirs[...]


def added(mine, theirs):
    outs = [(value.shape, BF16) for value in mine]
    return call(add_kernel, outs, [*mine, *theirs], 3 * mine[0].size, 0, "added")


def residual_kernel(scales, residual, partner_residual, grads, out, held, read, sems):
    rows, columns = residual.shape
    part = rows // OWN_STEPS
    parity = core_parity()
    work = []
    for side, source in ((0, residual), (1, partner_residual)):
        base = (parity if side == 0 else 1 - parity) * rows
        for step in range(OWN_STEPS):
            here = pl.ds(step * part, part)
            there = aligned(base + step * part, part)
            work.append(
                (
                    pltpu.make_async_copy(
                        grads.at[there], read.at[side, here], sems.at[0, side, step]
                    ),
                    pltpu.make_async_copy(
                        held.at[side, here], out.at[there], sems.at[1, side, step]
                    ),
                    side,
                    source,
                    here,
                    there,
                )
            )
            work[-1][0].start()
    for arrive, leave, side, source, here, there in work:
        arrive.wait()
        scale = scales[there, :]
        for block in range(columns // BLOCK):
            at = slice(block * BLOCK, (block + 1) * BLOCK)
            limit = scale[:, block : block + 1]
            summand = read[side, here, at].astype(F32) + source[here, at].astype(F32)
            kept = jnp.clip(summand.astype(BF16), -limit, limit)
            held[side, here, at] = (summand - kept.astype(F32)).astype(BF16)
        leave.start()
    for arrive, leave, *_ in work:
        leave.wait()


def new_residual(scales, residual, partner_residual, grads):
    rows, columns = residual.shape
    size = rows * columns
    return call(
        residual_kernel,
        [HbmOut((grads.shape, BF16))],
        [scales, residual, partner_residual, grads],
        12 * size,
        12 * size,
        "new_residual",
        scratch=[
            pltpu.VMEM((2, rows, columns), BF16),
            pltpu.VMEM((2, rows, columns), BF16),
            pltpu.SemaphoreType.DMA((2, 2, OWN_STEPS)),
        ],
        in_hbm=1,
    )[0]


def adam_kernel(flip_core, flip_cube, *refs):
    summed = refs[:PIECES]
    weight, moment_one, moment_two = refs[PIECES : PIECES + 3]
    outs = refs[-7:-4]
    held, sems = refs[-4:-1], refs[-1]
    _, half, width = held[0].shape
    parity = core_parity()
    parity = 1 - parity if flip_core else parity
    copies = []
    for piece in range(PIECES):
        bit = cube_bits()[piece]
        start = (1 - bit if flip_cube else bit) * half
        here = aligned(start, half)
        there = aligned(parity * 2 * half + start, half)
        for block in range(width // BLOCK):
            to = slice(block * BLOCK, (block + 1) * BLOCK)
            at = slice(piece * width + block * BLOCK, piece * width + (block + 1) * BLOCK)
            averaged = summed[piece][:, to].astype(F32) * (1.0 / 16.0)
            moment_a = BETA_ONE * moment_one[here, at] + (1.0 - BETA_ONE) * averaged
            moment_b = BETA_TWO * moment_two[here, at] + (1.0 - BETA_TWO) * averaged * averaged
            update = (LEARN_RATE / BIAS_ONE) * moment_a
            update = update / (jnp.sqrt(moment_b * (1.0 / BIAS_TWO)) + EPSILON)
            held[0][piece, :, to] = (weight[here, at].astype(F32) - update).astype(BF16)
            held[1][piece, :, to] = moment_a
            held[2][piece, :, to] = moment_b
        for kind in range(3):
            copies.append(
                pltpu.make_async_copy(
                    held[kind].at[piece],
                    outs[kind].at[there, pl.ds(piece * width, width)],
                    sems.at[kind, piece],
                )
            )
            copies[-1].start()
    for copy in copies:
        copy.wait()


def adam_quarter(flip_core, flip_cube, summed, weight, moment_one, moment_two, filled):
    rows, columns = weight.shape
    half, width = rows // 2, columns // PIECES
    kinds = (BF16, F32, F32)
    size = half * columns
    given = [*summed, weight, moment_one, moment_two]
    return call(
        functools.partial(adam_kernel, flip_core, flip_cube),
        [HbmOut(((2 * rows, columns), kind)) for kind in kinds],
        given + list(filled),
        30 * size,
        10 * size,
        "adam_quarter",
        scratch=[pltpu.VMEM((PIECES, half, width), kind) for kind in kinds]
        + [pltpu.SemaphoreType.DMA((3, PIECES))],
        aliases={len(given) + at: at for at in range(len(filled))},
        in_hbm=len(filled),
    )


def together(*values):
    return lax.optimization_barrier(values)


def shards(weight_old, moment_one, moment_two, residual_old, grads, exponents):
    residual = residual_old[0]
    grads = grads[0, 0]
    rows = residual.shape[0]
    exponents = exponents[0].transpose(2, 0, 1)

    message, scales = make_message(exponents, grads, rows)
    partner_message = core_swap(message)
    clipped, carried = clip_own(scales, grads, residual)
    sent, kept = pair_sums(clipped, carried, partner_message)

    def cube_step(sent, step):
        return [cube_swap(sent[piece], (piece + step) % 3) for piece in range(PIECES)]

    sent, residual, weight = together(sent, residual, weight_old)
    arrived = cube_step(sent, 0)
    arrived, partner_residual, partner_weight = together(
        arrived, core_swap(residual), core_swap(weight)
    )
    kept = added(kept, arrived)

    kept, one, two, partner_residual = together(kept, moment_one, moment_two, partner_residual)
    arrived = cube_step(kept, 1)
    left = new_residual(scales, carried, partner_residual, grads)
    arrived, partner_one, partner_two, left = together(
        arrived, core_swap(one), core_swap(two), left
    )
    kept = added(kept, arrived)

    arrived = cube_step(kept, 2)
    arrived = together(*arrived)
    kept = added(kept, arrived)

    own_old = (weight_old, moment_one, moment_two)
    partner_old = (partner_weight, partner_one, partner_two)
    gathered = cube_step(kept, 0)
    partner_kept = [core_swap(value) for value in kept]
    filled = adam_quarter(False, False, kept, *own_old, ())
    filled = adam_quarter(True, False, partner_kept, *partner_old, filled)
    gathered, filled = together(gathered, filled)
    partner_gathered = [core_swap(value) for value in gathered]
    filled = adam_quarter(False, True, gathered, *own_old, filled)
    filled = adam_quarter(True, True, partner_gathered, *partner_old, filled)
    return (filled[0][None], filled[1][None], filled[2][None], left[None, None])


def solution(mesh):
    in_specs = (
        P("section", None),
        P("section", None),
        P("section", None),
        P("dp", "section", None),
        P("dp", "section", None, None),
        P("dp", "section", None, None),
    )
    out_specs = (
        P("section", None, None),
        P("section", None, None),
        P("section", None, None),
        P("dp", "section", None, None),
    )
    return jax.shard_map(shards, mesh=mesh, in_specs=in_specs, out_specs=out_specs, check_vma=False)
```

```python
import functools

import jax
import jax.numpy as jnp
from jax import lax
from jax.experimental import pallas as pl
from jax.experimental.pallas import tpu as pltpu
from jax.sharding import PartitionSpec as P

BETA_ONE = 0.9
BETA_TWO = 0.95
LEARN_RATE = 0.001
EPSILON = 1e-08
BIAS_ONE = 1.0 - 0.9**10
BIAS_TWO = 1.0 - 0.95**10
BLOCK = 256
WIDTHS = (1280, 1024, 768)
STARTS = (0, 1280, 2304)
PIECES = len(WIDTHS)
LANES = 128
OWN_STEPS = 4
VMEM_LIMIT = 12 * 2**20
F32 = jnp.float32
BF16 = jnp.bfloat16
IN_VMEM = pl.BlockSpec(memory_space=pltpu.VMEM)
IN_HBM = pl.BlockSpec(memory_space=pltpu.HBM)


def core_swap(value):
    pairs = [(source, source ^ 1) for source in range(lax.axis_size("section"))]
    return lax.ppermute(value, "section", pairs)


def cube_swap(value, dim):
    count = lax.axis_size("dp")
    if dim == 0:
        pairs = [(source, source ^ 2) for source in range(count)]
    elif dim == 1:
        pairs = [(source, (3 - source // 2) * 2 + source % 2) for source in range(count)]
    else:
        pairs = [(source, source ^ 1) for source in range(count)]
    return lax.ppermute(value, "dp", pairs)


def core_parity():
    return lax.axis_index("section").astype(jnp.int32) % 2


def cube_bits():
    replica = lax.axis_index("dp").astype(jnp.int32)
    y = replica // 2
    return [((y + 1) // 2) % 2, y // 2, replica % 2]


class HbmOut(tuple):
    pass


def call(body, outs, operands, flops, moved, name, scratch=(), aliases=None, in_hbm=0):
    near = operands[: len(operands) - in_hbm]
    far = operands[len(operands) - in_hbm :]
    return pl.pallas_call(
        body,
        in_specs=[IN_VMEM] * len(near) + [IN_HBM] * in_hbm,
        out_specs=[IN_HBM if isinstance(out, HbmOut) else IN_VMEM for out in outs],
        out_shape=[
            (pltpu.HBM if isinstance(out, HbmOut) else pltpu.VMEM)(out[0], out[1]) for out in outs
        ],
        scratch_shapes=list(scratch),
        input_output_aliases=aliases or {},
        compiler_params=pltpu.CompilerParams(vmem_limit_bytes=VMEM_LIMIT),
        cost_estimate=pl.CostEstimate(flops=flops, bytes_accessed=moved, transcendentals=0),
        name=name,
    )(
        *[pltpu.with_memory_space_constraint(value, pltpu.VMEM) for value in near],
        *[pltpu.with_memory_space_constraint(value, pltpu.HBM) for value in far],
    )


def aligned(start, size):
    return pl.ds(pl.multiple_of(start, 32), size)


def message_kernel(exponents, grads, message, scales, read, turned, sems):
    rows, columns = message.shape[0], grads.shape[1]
    base = (1 - core_parity()) * rows
    part = rows // 4
    first = pltpu.make_async_copy(exponents, read, sems.at[4])
    first.start()
    copies = []
    for at in range(4):
        copies.append(
            pltpu.make_async_copy(
                grads.at[aligned(base + at * part, part)],
                message.at[pl.ds(at * part, part), pl.ds(0, columns)],
                sems.at[at],
            )
        )
        copies[-1].start()
    turned[...] = jnp.zeros_like(turned)
    first.wait()
    for block in range(exponents.shape[0]):
        turned[block : block + 1, :] = read[block].astype(F32)
    scales[...] = jnp.exp2(turned[...].T).astype(BF16)
    message[:, columns:] = scales[aligned(base, rows), :]
    for copy in copies:
        copy.wait()


def make_message(exponents, grads, rows):
    blocks, _, all_rows = exponents.shape
    columns = grads.shape[1]
    return call(
        message_kernel,
        [((rows, columns + LANES), BF16), ((all_rows, LANES), BF16)],
        [exponents, grads],
        0,
        2 * rows * columns,
        "make_message",
        scratch=[
            pltpu.VMEM(exponents.shape, exponents.dtype),
            pltpu.VMEM((LANES, all_rows), F32),
            pltpu.SemaphoreType.DMA((5,)),
        ],
        in_hbm=2,
    )


def own_kernel(scales, grads, residual, clipped, carried, read, sems):
    rows, columns = residual.shape
    base = core_parity() * rows
    part = rows // OWN_STEPS
    copies = []
    for step in range(OWN_STEPS):
        here = pl.ds(step * part, part)
        there = aligned(base + step * part, part)
        copies.append(
            (
                pltpu.make_async_copy(grads.at[there], read.at[here], sems.at[0, step]),
                pltpu.make_async_copy(residual.at[here], carried.at[here], sems.at[1, step]),
            )
        )
        for copy in copies[-1]:
            copy.start()
    for step in range(OWN_STEPS):
        for copy in copies[step]:
            copy.wait()
        here = slice(step * part, (step + 1) * part)
        scale = scales[aligned(base + step * part, part), :]
        for block in range(columns // BLOCK):
            at = slice(block * BLOCK, (block + 1) * BLOCK)
            limit = scale[:, block : block + 1]
            clipped[here, at] = jnp.clip(read[here, at] + carried[here, at], -limit, limit)


def clip_own(scales, grads, residual):
    rows, columns = residual.shape
    return call(
        own_kernel,
        [(residual.shape, BF16)] * 2,
        [scales, grads, residual],
        4 * rows * columns,
        4 * rows * columns,
        "clip_own",
        scratch=[pltpu.VMEM(residual.shape, BF16), pltpu.SemaphoreType.DMA((2, OWN_STEPS))],
        in_hbm=2,
    )


def pair_kernel(clipped, residual, message, *outs):
    rows, columns = residual.shape
    half = rows // 2
    bits = cube_bits()
    for piece, (first, width) in enumerate(zip(STARTS, WIDTHS)):
        for out, start in ((outs[piece], 1 - bits[piece]), (outs[PIECES + piece], bits[piece])):
            here = aligned(start * half, half)
            scale = message[here, columns:]
            for block in range(first // BLOCK, (first + width) // BLOCK):
                at = slice(block * BLOCK, (block + 1) * BLOCK)
                to = slice(block * BLOCK - first, (block + 1) * BLOCK - first)
                limit = scale[:, block : block + 1]
                partner = jnp.clip(message[here, at] + residual[here, at], -limit, limit)
                out[:, to] = clipped[here, at] + partner


def pair_sums(clipped, residual, message):
    rows, columns = residual.shape
    size = rows * columns
    outs = call(
        pair_kernel,
        [((rows // 2, width), BF16) for width in WIDTHS] * 2,
        [clipped, residual, message],
        5 * size,
        size,
        "pair_sums",
    )
    return outs[:PIECES], outs[PIECES:]


def add_kernel(*refs):
    packed = refs[3 * PIECES :]
    for piece, (first, width) in enumerate(zip(STARTS, WIDTHS)):
        total = refs[piece][...] + refs[PIECES + piece][...]
        refs[2 * PIECES + piece][...] = total
        for out in packed:
            out[:, first : first + width] = total


def added(mine, theirs, packed=False):
    outs = [(value.shape, BF16) for value in mine]
    if packed:
        outs.append(((mine[0].shape[0], sum(WIDTHS)), BF16))
    return call(add_kernel, outs, [*mine, *theirs], sum(value.size for value in mine), 0, "added")


def residual_kernel(flip_core, scales, residual, grads, *refs):
    out, held, read, sems = refs[-4:]
    rows, columns = residual.shape
    part = rows // OWN_STEPS
    parity = core_parity()
    base = (1 - parity if flip_core else parity) * rows
    work = []
    for step in range(OWN_STEPS):
        here = pl.ds(step * part, part)
        there = aligned(base + step * part, part)
        arrive = pltpu.make_async_copy(grads.at[there], read.at[here], sems.at[0, step])
        leave = pltpu.make_async_copy(held.at[here], out.at[there], sems.at[1, step])
        work.append((arrive, leave, here, there))
        arrive.start()
    for arrive, leave, here, there in work:
        arrive.wait()
        scale = scales[there, :]
        for block in range(columns // BLOCK):
            at = slice(block * BLOCK, (block + 1) * BLOCK)
            limit = scale[:, block : block + 1]
            summand = read[here, at].astype(F32) + residual[here, at].astype(F32)
            kept = jnp.clip(summand.astype(BF16), -limit, limit)
            held[here, at] = (summand - kept.astype(F32)).astype(BF16)
        leave.start()
    for _, leave, _, _ in work:
        leave.wait()


def residual_half(flip_core, scales, residual, grads, filled):
    rows, columns = residual.shape
    size = rows * columns
    return call(
        functools.partial(residual_kernel, flip_core),
        [HbmOut((grads.shape, BF16))],
        [scales, residual, grads, *filled],
        6 * size,
        4 * size,
        "residual_half",
        scratch=[
            pltpu.VMEM((rows, columns), BF16),
            pltpu.VMEM((rows, columns), BF16),
            pltpu.SemaphoreType.DMA((2, OWN_STEPS)),
        ],
        aliases={3: 0} if filled else {},
        in_hbm=1 + len(filled),
    )


def adam_kernel(flip_core, flip_cube, count, *refs):
    summed = refs[:count]
    weight, moment_one, moment_two = refs[count : count + 3]
    outs, held, sems = refs[-7:-4], refs[-4:-1], refs[-1]
    half = held[0].shape[0]
    parity = core_parity()
    parity = 1 - parity if flip_core else parity
    bits = cube_bits()
    copies = []
    for piece, (first, width) in enumerate(zip(STARTS, WIDTHS)):
        start = (1 - bits[piece] if flip_cube else bits[piece]) * half
        here = aligned(start, half)
        there = aligned(parity * 2 * half + start, half)
        for block in range(width // BLOCK):
            to = slice(block * BLOCK, (block + 1) * BLOCK)
            at = slice(first + block * BLOCK, first + (block + 1) * BLOCK)
            total = summed[0][:, at] if count == 1 else summed[piece][:, to]
            averaged = total.astype(F32) * (1.0 / 16.0)
            moment_a = BETA_ONE * moment_one[here, at] + (1.0 - BETA_ONE) * averaged
            moment_b = BETA_TWO * moment_two[here, at] + (1.0 - BETA_TWO) * averaged * averaged
            update = (LEARN_RATE / BIAS_ONE) * moment_a
            update = update / (jnp.sqrt(moment_b * (1.0 / BIAS_TWO)) + EPSILON)
            held[0][:, at] = (weight[here, at].astype(F32) - update).astype(BF16)
            held[1][:, at] = moment_a
            held[2][:, at] = moment_b
        at = pl.ds(first, width)
        for kind in range(3):
            copy = pltpu.make_async_copy(
                held[kind].at[:, at], outs[kind].at[there, at], sems.at[kind, piece]
            )
            copy.start()
            copies.append(copy)
    for copy in copies:
        copy.wait()


def adam_quarter(flip_core, flip_cube, summed, weight, moment_one, moment_two, filled):
    rows, columns = weight.shape
    half = rows // 2
    kinds = (BF16, F32, F32)
    size = half * columns
    given = [*summed, weight, moment_one, moment_two]
    return call(
        functools.partial(adam_kernel, flip_core, flip_cube, len(summed)),
        [HbmOut(((2 * rows, columns), kind)) for kind in kinds],
        given + list(filled),
        30 * size,
        10 * size,
        "adam_quarter",
        scratch=[pltpu.VMEM((half, columns), kind) for kind in kinds]
        + [pltpu.SemaphoreType.DMA((3, PIECES))],
        aliases={len(given) + at: at for at in range(len(filled))},
        in_hbm=len(filled),
    )


def together(*values):
    return lax.optimization_barrier(values)


def shards(weight_old, moment_one, moment_two, residual_old, grads, exponents):
    residual = residual_old[0]
    grads = grads[0, 0]
    rows = residual.shape[0]
    exponents = exponents[0].transpose(2, 0, 1)

    message, scales = make_message(exponents, grads, rows)
    partner_message = core_swap(message)
    clipped, carried = clip_own(scales, grads, residual)
    held, weight = together(carried, weight_old)
    partner_residual, partner_weight = core_swap(held), core_swap(weight)
    sent, kept = pair_sums(clipped, carried, partner_message)

    def cube_step(sent, step):
        return [cube_swap(sent[piece], (piece + step) % 3) for piece in range(PIECES)]

    sent, carried = together(sent, carried)
    arrived = cube_step(sent, 0)
    left = residual_half(False, scales, carried, grads, ())
    arrived, left, partner_residual, partner_weight = together(
        arrived, left, partner_residual, partner_weight
    )
    kept = added(kept, arrived)

    kept, one, two, partner_residual = together(kept, moment_one, moment_two, partner_residual)
    arrived = cube_step(kept, 1)
    left = residual_half(True, scales, partner_residual, grads, left)
    arrived, left, partner_one, partner_two = together(
        arrived, left, core_swap(one), core_swap(two)
    )
    kept = added(kept, arrived)

    arrived = together(*cube_step(kept, 2))
    *kept, packed = added(kept, arrived, packed=True)

    own_old = (weight_old, moment_one, moment_two)
    partner_old = (partner_weight, partner_one, partner_two)
    gathered = cube_step(kept, 0)
    partner_packed = core_swap(packed)
    filled = adam_quarter(False, False, kept, *own_old, ())
    filled = adam_quarter(True, False, [partner_packed], *partner_old, filled)
    gathered, filled = together(gathered, filled)
    partner_gathered = [core_swap(value) for value in gathered]
    filled = adam_quarter(False, True, gathered, *own_old, filled)
    filled = adam_quarter(True, True, partner_gathered, *partner_old, filled)
    return (filled[0][None], filled[1][None], filled[2][None], left[0][None, None])


def solution(mesh):
    in_specs = (
        P("section", None),
        P("section", None),
        P("section", None),
        P("dp", "section", None),
        P("dp", "section", None, None),
        P("dp", "section", None, None),
    )
    out_specs = (
        P("section", None, None),
        P("section", None, None),
        P("section", None, None),
        P("dp", "section", None, None),
    )
    return jax.shard_map(shards, mesh=mesh, in_specs=in_specs, out_specs=out_specs, check_vma=False)
```

```python
import functools

import jax
import jax.numpy as jnp
from jax import lax
from jax.experimental import pallas as pl
from jax.experimental.pallas import tpu as pltpu
from jax.sharding import PartitionSpec as P

BETA_ONE = 0.9
BETA_TWO = 0.95
LEARN_RATE = 0.001
EPSILON = 1e-08
BIAS_ONE = 1.0 - 0.9**10
BIAS_TWO = 1.0 - 0.95**10
BLOCK = 256
WIDTHS = (1024, 1024, 1024)
STARTS = (0, 1024, 2048)
PIECES = len(WIDTHS)
LANES = 128
OWN_STEPS = 4
VMEM_LIMIT = 12 * 2**20
F32 = jnp.float32
BF16 = jnp.bfloat16
IN_VMEM = pl.BlockSpec(memory_space=pltpu.VMEM)
IN_HBM = pl.BlockSpec(memory_space=pltpu.HBM)


def core_swap(value):
    pairs = [(source, source ^ 1) for source in range(lax.axis_size("section"))]
    return lax.ppermute(value, "section", pairs)


def cube_partner(replica, dim):
    if dim == 0:
        return replica ^ 2
    if dim == 1:
        return (3 - replica // 2) * 2 + replica % 2
    return replica ^ 1


def core_dim(dim, parity):
    return (dim + 2 * parity) % 3


def cube_swap(value, dim):
    replicas = lax.axis_size("dp")
    pairs = []
    for section in range(lax.axis_size("section")):
        for replica in range(replicas):
            to = cube_partner(replica, core_dim(dim, section % 2))
            pairs.append((section * replicas + replica, section * replicas + to))
    return lax.ppermute(value, ("section", "dp"), pairs)


def core_parity():
    return lax.axis_index("section").astype(jnp.int32) % 2


def cube_bits(parity):
    replica = lax.axis_index("dp").astype(jnp.int32)
    y = replica // 2
    bits = [((y + 1) // 2) % 2, y // 2, replica % 2]
    return [
        jnp.where(parity == 0, bits[core_dim(piece, 0)], bits[core_dim(piece, 1)])
        for piece in range(PIECES)
    ]


class HbmOut(tuple):
    pass


def call(body, outs, operands, flops, moved, name, scratch=(), aliases=None, in_hbm=0):
    near = operands[: len(operands) - in_hbm]
    far = operands[len(operands) - in_hbm :]
    return pl.pallas_call(
        body,
        in_specs=[IN_VMEM] * len(near) + [IN_HBM] * in_hbm,
        out_specs=[IN_HBM if isinstance(out, HbmOut) else IN_VMEM for out in outs],
        out_shape=[
            (pltpu.HBM if isinstance(out, HbmOut) else pltpu.VMEM)(out[0], out[1]) for out in outs
        ],
        scratch_shapes=list(scratch),
        input_output_aliases=aliases or {},
        compiler_params=pltpu.CompilerParams(vmem_limit_bytes=VMEM_LIMIT),
        cost_estimate=pl.CostEstimate(flops=flops, bytes_accessed=moved, transcendentals=0),
        name=name,
    )(
        *[pltpu.with_memory_space_constraint(value, pltpu.VMEM) for value in near],
        *[pltpu.with_memory_space_constraint(value, pltpu.HBM) for value in far],
    )


def aligned(start, size):
    return pl.ds(pl.multiple_of(start, 32), size)


def message_kernel(exponents, grads, message, scales, read, turned, sems):
    rows, columns = message.shape[0], grads.shape[1]
    base = (1 - core_parity()) * rows
    part = rows // 4
    first = pltpu.make_async_copy(exponents, read, sems.at[4])
    first.start()
    copies = []
    for at in range(4):
        copies.append(
            pltpu.make_async_copy(
                grads.at[aligned(base + at * part, part)],
                message.at[pl.ds(at * part, part), pl.ds(0, columns)],
                sems.at[at],
            )
        )
        copies[-1].start()
    turned[...] = jnp.zeros_like(turned)
    first.wait()
    for block in range(exponents.shape[0]):
        turned[block : block + 1, :] = read[block].astype(F32)
    scales[...] = jnp.exp2(turned[...].T).astype(BF16)
    message[:, columns:] = scales[aligned(base, rows), :]
    for copy in copies:
        copy.wait()


def make_message(exponents, grads, rows):
    blocks, _, all_rows = exponents.shape
    columns = grads.shape[1]
    return call(
        message_kernel,
        [((rows, columns + LANES), BF16), ((all_rows, LANES), BF16)],
        [exponents, grads],
        0,
        2 * rows * columns,
        "make_message",
        scratch=[
            pltpu.VMEM(exponents.shape, exponents.dtype),
            pltpu.VMEM((LANES, all_rows), F32),
            pltpu.SemaphoreType.DMA((5,)),
        ],
        in_hbm=2,
    )


def own_kernel(scales, grads, residual, clipped, carried, read, sems):
    rows, columns = residual.shape
    base = core_parity() * rows
    part = rows // OWN_STEPS
    copies = []
    for step in range(OWN_STEPS):
        here = pl.ds(step * part, part)
        there = aligned(base + step * part, part)
        copies.append(
            (
                pltpu.make_async_copy(grads.at[there], read.at[here], sems.at[0, step]),
                pltpu.make_async_copy(residual.at[here], carried.at[here], sems.at[1, step]),
            )
        )
        for copy in copies[-1]:
            copy.start()
    for step in range(OWN_STEPS):
        for copy in copies[step]:
            copy.wait()
        here = slice(step * part, (step + 1) * part)
        scale = scales[aligned(base + step * part, part), :]
        for block in range(columns // BLOCK):
            at = slice(block * BLOCK, (block + 1) * BLOCK)
            limit = scale[:, block : block + 1]
            clipped[here, at] = jnp.clip(read[here, at] + carried[here, at], -limit, limit)


def clip_own(scales, grads, residual):
    rows, columns = residual.shape
    return call(
        own_kernel,
        [(residual.shape, BF16)] * 2,
        [scales, grads, residual],
        4 * rows * columns,
        4 * rows * columns,
        "clip_own",
        scratch=[pltpu.VMEM(residual.shape, BF16), pltpu.SemaphoreType.DMA((2, OWN_STEPS))],
        in_hbm=2,
    )


def pair_kernel(flip_cube, clipped, residual, message, *outs):
    rows, columns = residual.shape
    half = rows // 2
    bits = cube_bits(core_parity())
    for out, bit, first, width in zip(outs, bits, STARTS, WIDTHS):
        here = aligned((1 - bit if flip_cube else bit) * half, half)
        scale = message[here, columns:]
        for block in range(first // BLOCK, (first + width) // BLOCK):
            at = slice(block * BLOCK, (block + 1) * BLOCK)
            to = slice(block * BLOCK - first, (block + 1) * BLOCK - first)
            limit = scale[:, block : block + 1]
            partner = jnp.clip(message[here, at] + residual[here, at], -limit, limit)
            out[:, to] = clipped[here, at] + partner


def pair_sums(flip_cube, clipped, residual, message):
    rows, columns = residual.shape
    size = rows * columns // 2
    return call(
        functools.partial(pair_kernel, flip_cube),
        [((rows // 2, width), BF16) for width in WIDTHS],
        [clipped, residual, message],
        5 * size,
        size,
        "pair_sums",
    )


def pack_kernel(*refs):
    for part, first, width in zip(refs, STARTS, WIDTHS):
        refs[-1][:, first : first + width] = part[...]


def packed_pieces(parts):
    shape = (parts[0].shape[0], sum(WIDTHS))
    return call(pack_kernel, [(shape, BF16)], parts, 0, 0, "pack")[0]


def add_kernel(mine, theirs, out):
    out[...] = mine[...] + theirs[...]


def added(mine, theirs):
    return call(add_kernel, [(mine.shape, BF16)], [mine, theirs], mine.size, 0, "added")[0]


def residual_kernel(flip_core, scales, residual, grads, *refs):
    out, held, read, sems = refs[-4:]
    rows, columns = residual.shape
    part = rows // OWN_STEPS
    parity = core_parity()
    base = (1 - parity if flip_core else parity) * rows
    work = []
    for step in range(OWN_STEPS):
        here = pl.ds(step * part, part)
        there = aligned(base + step * part, part)
        arrive = pltpu.make_async_copy(grads.at[there], read.at[here], sems.at[0, step])
        leave = pltpu.make_async_copy(held.at[here], out.at[there], sems.at[1, step])
        work.append((arrive, leave, here, there))
        arrive.start()
    for arrive, leave, here, there in work:
        arrive.wait()
        scale = scales[there, :]
        for block in range(columns // BLOCK):
            at = slice(block * BLOCK, (block + 1) * BLOCK)
            limit = scale[:, block : block + 1]
            summand = read[here, at].astype(F32) + residual[here, at].astype(F32)
            kept = jnp.clip(summand.astype(BF16), -limit, limit)
            held[here, at] = (summand - kept.astype(F32)).astype(BF16)
        leave.start()
    for _, leave, _, _ in work:
        leave.wait()


def residual_half(flip_core, scales, residual, grads, filled):
    rows, columns = residual.shape
    size = rows * columns
    return call(
        functools.partial(residual_kernel, flip_core),
        [HbmOut((grads.shape, BF16))],
        [scales, residual, grads, *filled],
        6 * size,
        4 * size,
        "residual_half",
        scratch=[
            pltpu.VMEM((rows, columns), BF16),
            pltpu.VMEM((rows, columns), BF16),
            pltpu.SemaphoreType.DMA((2, OWN_STEPS)),
        ],
        aliases={3: 0} if filled else {},
        in_hbm=1 + len(filled),
    )


def adam_kernel(jobs, *refs):
    outs, held, sems = refs[-7:-4], refs[-4:-1], refs[-1]
    half = held[0].shape[1]
    copies = []
    used = 0
    for job, (flip_core, flip_cube, count) in enumerate(jobs):
        summed = refs[used : used + count]
        weight, moment_one, moment_two = refs[used + count : used + count + 3]
        used += count + 3
        parity = core_parity()
        parity = 1 - parity if flip_core else parity
        bits = cube_bits(parity)
        for piece, (first, width) in enumerate(zip(STARTS, WIDTHS)):
            start = (1 - bits[piece] if flip_cube else bits[piece]) * half
            here = aligned(start, half)
            there = aligned(parity * 2 * half + start, half)
            for block in range(width // BLOCK):
                to = slice(block * BLOCK, (block + 1) * BLOCK)
                at = slice(first + block * BLOCK, first + (block + 1) * BLOCK)
                total = summed[0][:, at] if count == 1 else summed[piece][:, to]
                averaged = total.astype(F32) * (1.0 / 16.0)
                moment_a = BETA_ONE * moment_one[here, at] + (1.0 - BETA_ONE) * averaged
                moment_b = BETA_TWO * moment_two[here, at]
                moment_b = moment_b + (1.0 - BETA_TWO) * averaged * averaged
                update = (LEARN_RATE / BIAS_ONE) * moment_a
                update = update / (jnp.sqrt(moment_b * (1.0 / BIAS_TWO)) + EPSILON)
                held[0][job, :, at] = (weight[here, at].astype(F32) - update).astype(BF16)
                held[1][job, :, at] = moment_a
                held[2][job, :, at] = moment_b
            at = pl.ds(first, width)
            for kind in range(3):
                copy = pltpu.make_async_copy(
                    held[kind].at[job, :, at], outs[kind].at[there, at], sems.at[job, kind, piece]
                )
                copy.start()
                copies.append(copy)
    for copy in copies:
        copy.wait()


def adam(jobs, filled):
    rows, columns = jobs[0][3][0].shape
    half = rows // 2
    kinds = (BF16, F32, F32)
    size = len(jobs) * half * columns
    given = [value for _, _, summed, old in jobs for value in (*summed, *old)]
    return call(
        functools.partial(adam_kernel, [(core, cube, len(sums)) for core, cube, sums, _ in jobs]),
        [HbmOut(((2 * rows, columns), kind)) for kind in kinds],
        given + list(filled),
        30 * size,
        10 * size,
        "adam",
        scratch=[pltpu.VMEM((len(jobs), half, columns), kind) for kind in kinds]
        + [pltpu.SemaphoreType.DMA((len(jobs), 3, PIECES))],
        aliases={len(given) + at: at for at in range(len(filled))},
        in_hbm=len(filled),
    )


def together(*values):
    return lax.optimization_barrier(values)


def shards(weight_old, moment_one, moment_two, residual_old, grads, exponents):
    residual = residual_old[0]
    grads = grads[0, 0]
    rows = residual.shape[0]
    exponents = exponents[0].transpose(2, 0, 1)

    message, scales = make_message(exponents, grads, rows)
    partner_message = core_swap(message)
    clipped, carried = clip_own(scales, grads, residual)
    held, weight = together(carried, weight_old)
    partner_residual, partner_weight = core_swap(held), core_swap(weight)
    sent = pair_sums(True, clipped, carried, partner_message)
    sent, carried, clipped = together(sent, carried, clipped)
    kept = list(pair_sums(False, clipped, carried, partner_message))
    left = residual_half(False, scales, carried, grads, ())
    sent = list(sent)
    last = PIECES - 1
    arrived = [cube_swap(sent[piece], piece) for piece in range(PIECES)]
    arrived, kept, left, partner_residual, partner_weight = together(
        arrived, kept, left, partner_residual, partner_weight
    )
    kept = [added(*pair) for pair in zip(kept, arrived)]
    kept, one, two, partner_residual = together(kept, moment_one, moment_two, partner_residual)
    partner_one, partner_two = core_swap(one), core_swap(two)
    left = residual_half(True, scales, partner_residual, grads, left)
    arrived = [cube_swap(kept[piece], piece + 1) for piece in range(PIECES)]
    arrived[last], left = together(arrived[last], left)
    kept = [added(*pair) for pair in zip(kept, arrived)]
    arrived = [cube_swap(kept[piece], piece + 2) for piece in range(PIECES)]
    arrived[last], partner_one, partner_two = together(arrived[last], partner_one, partner_two)
    kept = [added(*pair) for pair in zip(kept, arrived)]

    own_old = (weight_old, moment_one, moment_two)
    partner_old = (partner_weight, partner_one, partner_two)
    gathered = [cube_swap(kept[piece], piece) for piece in range(PIECES)]
    partner_packed = core_swap(packed_pieces(kept))
    filled = adam([(False, False, kept, own_old)], ())
    gathered, filled = together(gathered, filled)
    partner_gathered = core_swap(packed_pieces(gathered))
    filled = adam([(True, False, [partner_packed], partner_old)], filled)
    filled = adam(
        [(False, True, gathered, own_old), (True, True, [partner_gathered], partner_old)], filled
    )
    return (filled[0][None], filled[1][None], filled[2][None], left[0][None, None])


def solution(mesh):
    in_specs = (
        P("section", None),
        P("section", None),
        P("section", None),
        P("dp", "section", None),
        P("dp", "section", None, None),
        P("dp", "section", None, None),
    )
    out_specs = (
        P("section", None, None),
        P("section", None, None),
        P("section", None, None),
        P("dp", "section", None, None),
    )
    return jax.shard_map(shards, mesh=mesh, in_specs=in_specs, out_specs=out_specs, check_vma=False)
```

```python
import functools

import jax
import jax.numpy as jnp
from jax import lax
from jax.experimental import pallas as pl
from jax.experimental.pallas import tpu as pltpu
from jax.sharding import PartitionSpec as P

BETA_ONE = 0.9
BETA_TWO = 0.95
LEARN_RATE = 0.001
EPSILON = 1e-08
BIAS_ONE = 1.0 - 0.9**10
BIAS_TWO = 1.0 - 0.95**10
BLOCK = 256
WIDTHS = (1024, 1024, 1024)
STARTS = (0, 1024, 2048)
PIECES = len(WIDTHS)
LANES = 128
OWN_STEPS = 4
VMEM_LIMIT = 12 * 2**20
F32 = jnp.float32
BF16 = jnp.bfloat16
IN_VMEM = pl.BlockSpec(memory_space=pltpu.VMEM)
IN_HBM = pl.BlockSpec(memory_space=pltpu.HBM)


def core_swap(value):
    pairs = [(source, source ^ 1) for source in range(lax.axis_size("section"))]
    return lax.ppermute(value, "section", pairs)


def cube_partner(replica, dim):
    if dim == 0:
        return replica ^ 2
    if dim == 1:
        return (3 - replica // 2) * 2 + replica % 2
    return replica ^ 1


def core_dim(dim, parity):
    return (dim + 2 * parity) % 3


def cube_swap(value, dim):
    replicas = lax.axis_size("dp")
    pairs = []
    for section in range(lax.axis_size("section")):
        for replica in range(replicas):
            to = cube_partner(replica, core_dim(dim, section % 2))
            pairs.append((section * replicas + replica, section * replicas + to))
    return lax.ppermute(value, ("section", "dp"), pairs)


def core_parity():
    return lax.axis_index("section").astype(jnp.int32) % 2


def cube_bits(parity):
    replica = lax.axis_index("dp").astype(jnp.int32)
    y = replica // 2
    bits = [((y + 1) // 2) % 2, y // 2, replica % 2]
    return [
        jnp.where(parity == 0, bits[core_dim(piece, 0)], bits[core_dim(piece, 1)])
        for piece in range(PIECES)
    ]


class HbmOut(tuple):
    pass


def call(body, outs, operands, flops, moved, name, scratch=(), aliases=None, in_hbm=0):
    near = operands[: len(operands) - in_hbm]
    far = operands[len(operands) - in_hbm :]
    return pl.pallas_call(
        body,
        in_specs=[IN_VMEM] * len(near) + [IN_HBM] * in_hbm,
        out_specs=[IN_HBM if isinstance(out, HbmOut) else IN_VMEM for out in outs],
        out_shape=[
            (pltpu.HBM if isinstance(out, HbmOut) else pltpu.VMEM)(out[0], out[1]) for out in outs
        ],
        scratch_shapes=list(scratch),
        input_output_aliases=aliases or {},
        compiler_params=pltpu.CompilerParams(vmem_limit_bytes=VMEM_LIMIT),
        cost_estimate=pl.CostEstimate(flops=flops, bytes_accessed=moved, transcendentals=0),
        name=name,
    )(
        *[pltpu.with_memory_space_constraint(value, pltpu.VMEM) for value in near],
        *[pltpu.with_memory_space_constraint(value, pltpu.HBM) for value in far],
    )


def aligned(start, size):
    return pl.ds(pl.multiple_of(start, 32), size)


def message_kernel(exponents, grads, message, scales, read, turned, sems):
    rows, columns = message.shape[0], grads.shape[1]
    base = (1 - core_parity()) * rows
    part = rows // 4
    first = pltpu.make_async_copy(exponents, read, sems.at[4])
    first.start()
    copies = []
    for at in range(4):
        copies.append(
            pltpu.make_async_copy(
                grads.at[aligned(base + at * part, part)],
                message.at[pl.ds(at * part, part), pl.ds(0, columns)],
                sems.at[at],
            )
        )
        copies[-1].start()
    turned[...] = jnp.zeros_like(turned)
    first.wait()
    for block in range(exponents.shape[0]):
        turned[block : block + 1, :] = read[block].astype(F32)
    scales[...] = jnp.exp2(turned[...].T).astype(BF16)
    message[:, columns:] = scales[aligned(base, rows), :]
    for copy in copies:
        copy.wait()


def make_message(exponents, grads, rows):
    blocks, _, all_rows = exponents.shape
    columns = grads.shape[1]
    return call(
        message_kernel,
        [((rows, columns + LANES), BF16), ((all_rows, LANES), BF16)],
        [exponents, grads],
        0,
        2 * rows * columns,
        "make_message",
        scratch=[
            pltpu.VMEM(exponents.shape, exponents.dtype),
            pltpu.VMEM((LANES, all_rows), F32),
            pltpu.SemaphoreType.DMA((5,)),
        ],
        in_hbm=2,
    )


def own_kernel(scales, grads, residual, clipped, carried, read, sems):
    rows, columns = residual.shape
    base = core_parity() * rows
    part = rows // OWN_STEPS
    copies = []
    for step in range(OWN_STEPS):
        here = pl.ds(step * part, part)
        there = aligned(base + step * part, part)
        copies.append(
            (
                pltpu.make_async_copy(grads.at[there], read.at[here], sems.at[0, step]),
                pltpu.make_async_copy(residual.at[here], carried.at[here], sems.at[1, step]),
            )
        )
        for copy in copies[-1]:
            copy.start()
    for step in range(OWN_STEPS):
        for copy in copies[step]:
            copy.wait()
        here = slice(step * part, (step + 1) * part)
        scale = scales[aligned(base + step * part, part), :]
        for block in range(columns // BLOCK):
            at = slice(block * BLOCK, (block + 1) * BLOCK)
            limit = scale[:, block : block + 1]
            clipped[here, at] = jnp.clip(read[here, at] + carried[here, at], -limit, limit)


def clip_own(scales, grads, residual):
    rows, columns = residual.shape
    return call(
        own_kernel,
        [(residual.shape, BF16)] * 2,
        [scales, grads, residual],
        4 * rows * columns,
        4 * rows * columns,
        "clip_own",
        scratch=[pltpu.VMEM(residual.shape, BF16), pltpu.SemaphoreType.DMA((2, OWN_STEPS))],
        in_hbm=2,
    )


def pair_kernel(flip_cube, pieces, clipped, residual, message, *outs):
    rows, columns = residual.shape
    half = rows // 2
    bits = cube_bits(core_parity())
    for out, piece in zip(outs, pieces):
        bit, first, width = bits[piece], STARTS[piece], WIDTHS[piece]
        here = aligned((1 - bit if flip_cube else bit) * half, half)
        scale = message[here, columns:]
        for block in range(first // BLOCK, (first + width) // BLOCK):
            at = slice(block * BLOCK, (block + 1) * BLOCK)
            to = slice(block * BLOCK - first, (block + 1) * BLOCK - first)
            limit = scale[:, block : block + 1]
            partner = jnp.clip(message[here, at] + residual[here, at], -limit, limit)
            out[:, to] = clipped[here, at] + partner


def pair_sums(flip_cube, pieces, clipped, residual, message):
    rows, columns = residual.shape
    size = rows * columns // 2
    return call(
        functools.partial(pair_kernel, flip_cube, pieces),
        [((rows // 2, WIDTHS[piece]), BF16) for piece in pieces],
        [clipped, residual, message],
        5 * size,
        size,
        "pair_sums",
    )


def pack_kernel(*refs):
    for part, first, width in zip(refs, STARTS, WIDTHS):
        refs[-1][:, first : first + width] = part[...]


def packed_pieces(parts):
    shape = (parts[0].shape[0], sum(WIDTHS))
    return call(pack_kernel, [(shape, BF16)], parts, 0, 0, "pack")[0]


def add_kernel(mine, theirs, out):
    out[...] = mine[...] + theirs[...]


def added(mine, theirs):
    return call(add_kernel, [(mine.shape, BF16)], [mine, theirs], mine.size, 0, "added")[0]


def residual_kernel(flip_core, scales, residual, grads, *refs):
    out, held, read, sems = refs[-4:]
    rows, columns = residual.shape
    part = rows // OWN_STEPS
    parity = core_parity()
    base = (1 - parity if flip_core else parity) * rows
    work = []
    for step in range(OWN_STEPS):
        here = pl.ds(step * part, part)
        there = aligned(base + step * part, part)
        arrive = pltpu.make_async_copy(grads.at[there], read.at[here], sems.at[0, step])
        leave = pltpu.make_async_copy(held.at[here], out.at[there], sems.at[1, step])
        work.append((arrive, leave, here, there))
        arrive.start()
    for arrive, leave, here, there in work:
        arrive.wait()
        scale = scales[there, :]
        for block in range(columns // BLOCK):
            at = slice(block * BLOCK, (block + 1) * BLOCK)
            limit = scale[:, block : block + 1]
            summand = read[here, at].astype(F32) + residual[here, at].astype(F32)
            kept = jnp.clip(summand.astype(BF16), -limit, limit)
            held[here, at] = (summand - kept.astype(F32)).astype(BF16)
        leave.start()
    for _, leave, _, _ in work:
        leave.wait()


def residual_half(flip_core, scales, residual, grads, filled):
    rows, columns = residual.shape
    size = rows * columns
    return call(
        functools.partial(residual_kernel, flip_core),
        [HbmOut((grads.shape, BF16))],
        [scales, residual, grads, *filled],
        6 * size,
        4 * size,
        "residual_half",
        scratch=[
            pltpu.VMEM((rows, columns), BF16),
            pltpu.VMEM((rows, columns), BF16),
            pltpu.SemaphoreType.DMA((2, OWN_STEPS)),
        ],
        aliases={3: 0} if filled else {},
        in_hbm=1 + len(filled),
    )


def adam_kernel(jobs, *refs):
    outs, held, sems = refs[-7:-4], refs[-4:-1], refs[-1]
    half = held[0].shape[1]
    copies = []
    used = 0
    for job, (flip_core, flip_cube, count) in enumerate(jobs):
        summed = refs[used : used + count]
        weight, moment_one, moment_two = refs[used + count : used + count + 3]
        used += count + 3
        parity = core_parity()
        parity = 1 - parity if flip_core else parity
        bits = cube_bits(parity)
        for piece, (first, width) in enumerate(zip(STARTS, WIDTHS)):
            start = (1 - bits[piece] if flip_cube else bits[piece]) * half
            here = aligned(start, half)
            there = aligned(parity * 2 * half + start, half)
            for block in range(width // BLOCK):
                to = slice(block * BLOCK, (block + 1) * BLOCK)
                at = slice(first + block * BLOCK, first + (block + 1) * BLOCK)
                total = summed[0][:, at] if count == 1 else summed[piece][:, to]
                averaged = total.astype(F32) * (1.0 / 16.0)
                moment_a = BETA_ONE * moment_one[here, at] + (1.0 - BETA_ONE) * averaged
                moment_b = BETA_TWO * moment_two[here, at]
                moment_b = moment_b + (1.0 - BETA_TWO) * averaged * averaged
                update = (LEARN_RATE / BIAS_ONE) * moment_a
                update = update / (jnp.sqrt(moment_b * (1.0 / BIAS_TWO)) + EPSILON)
                held[0][job, :, at] = (weight[here, at].astype(F32) - update).astype(BF16)
                held[1][job, :, at] = moment_a
                held[2][job, :, at] = moment_b
            at = pl.ds(first, width)
            for kind in range(3):
                copy = pltpu.make_async_copy(
                    held[kind].at[job, :, at], outs[kind].at[there, at], sems.at[job, kind, piece]
                )
                copy.start()
                copies.append(copy)
    for copy in copies:
        copy.wait()


def adam(jobs, filled):
    rows, columns = jobs[0][3][0].shape
    half = rows // 2
    kinds = (BF16, F32, F32)
    size = len(jobs) * half * columns
    given = [value for _, _, summed, old in jobs for value in (*summed, *old)]
    return call(
        functools.partial(adam_kernel, [(core, cube, len(sums)) for core, cube, sums, _ in jobs]),
        [HbmOut(((2 * rows, columns), kind)) for kind in kinds],
        given + list(filled),
        30 * size,
        10 * size,
        "adam",
        scratch=[pltpu.VMEM((len(jobs), half, columns), kind) for kind in kinds]
        + [pltpu.SemaphoreType.DMA((len(jobs), 3, PIECES))],
        aliases={len(given) + at: at for at in range(len(filled))},
        in_hbm=len(filled),
    )


def together(*values):
    return lax.optimization_barrier(values)


def shards(weight_old, moment_one, moment_two, residual_old, grads, exponents):
    residual = residual_old[0]
    grads = grads[0, 0]
    rows = residual.shape[0]
    exponents = exponents[0].transpose(2, 0, 1)

    message, scales = make_message(exponents, grads, rows)
    partner_message = core_swap(message)
    clipped, carried = clip_own(scales, grads, residual)
    held, weight = together(carried, weight_old)
    partner_residual, partner_weight = core_swap(held), core_swap(weight)
    pieces = range(PIECES)
    sent = [pair_sums(True, [piece], clipped, carried, partner_message)[0] for piece in pieces]
    sent[-1], carried, clipped = together(sent[-1], carried, clipped)
    kept = list(pair_sums(False, list(pieces), clipped, carried, partner_message))
    left = residual_half(False, scales, carried, grads, ())
    sent = list(sent)
    last = PIECES - 1
    arrived = [cube_swap(sent[piece], piece) for piece in range(PIECES)]
    arrived, kept, left, partner_residual, partner_weight = together(
        arrived, kept, left, partner_residual, partner_weight
    )
    kept = [added(*pair) for pair in zip(kept, arrived)]
    kept, one, two, partner_residual = together(kept, moment_one, moment_two, partner_residual)
    partner_one, partner_two = core_swap(one), core_swap(two)
    left = residual_half(True, scales, partner_residual, grads, left)
    arrived = [cube_swap(kept[piece], piece + 1) for piece in range(PIECES)]
    arrived[last], left = together(arrived[last], left)
    kept = [added(*pair) for pair in zip(kept, arrived)]
    arrived = [cube_swap(kept[piece], piece + 2) for piece in range(PIECES)]
    arrived[last], partner_one, partner_two = together(arrived[last], partner_one, partner_two)
    kept = [added(*pair) for pair in zip(kept, arrived)]

    own_old = (weight_old, moment_one, moment_two)
    partner_old = (partner_weight, partner_one, partner_two)
    gathered = [cube_swap(kept[piece], piece) for piece in range(PIECES)]
    partner_packed = core_swap(packed_pieces(kept))
    filled = adam([(False, False, kept, own_old)], ())
    gathered, filled = together(gathered, filled)
    partner_gathered = core_swap(packed_pieces(gathered))
    filled = adam([(True, False, [partner_packed], partner_old)], filled)
    filled = adam(
        [(False, True, gathered, own_old), (True, True, [partner_gathered], partner_old)], filled
    )
    return (filled[0][None], filled[1][None], filled[2][None], left[0][None, None])


def solution(mesh):
    in_specs = (
        P("section", None),
        P("section", None),
        P("section", None),
        P("dp", "section", None),
        P("dp", "section", None, None),
        P("dp", "section", None, None),
    )
    out_specs = (
        P("section", None, None),
        P("section", None, None),
        P("section", None, None),
        P("dp", "section", None, None),
    )
    return jax.shard_map(shards, mesh=mesh, in_specs=in_specs, out_specs=out_specs, check_vma=False)
```
